256 devices in a mesh: fsdp: 16 (over z, x_hi), tp: 16 (over x_lo, y, core).
Axes of the slice: x: 4 (x_hi: 2, x_lo: 2; x = x_hi * 2 + x_lo), y: 4, z: 8, core: 2. Of those that a mesh axis runs over, the one named last changes fastest.
Arguments:
- attention_output: bfloat16 [8192, 8192], P('fsdp', 'tp'), may hold values from -6 to 6
- grad_out: bfloat16 [8192, 8192], P('fsdp', 'tp'), may hold values from -6 to 6
- base_weight: bfloat16 [8192, 8192], P('tp', 'fsdp'), may hold values from -0.0625 to 0.0625
- adapter_down: bfloat16 [8, 8192, 64], P(None, 'tp'), may hold values from -0.0625 to 0.0625
- adapter_up: bfloat16 [8, 64, 8192], P(None, None, 'tp'), may hold values from -0.0625 to 0.0625
- roles: int32 [64, 1], P('fsdp'), may hold values from 0 to 7
- live: int32 [64], P('fsdp'), may hold values 0 or 1
Outputs:
- input_gradient: bfloat16 [8192, 8192], P('fsdp', 'tp')
- down_gradient: float32 [8, 8192, 64], P(None, 'tp')
- up_gradient: float32 [8, 64, 8192], P(None, None, 'tp')
The draws below stay inside these ranges and needn't reach their ends.
Inputs may be any that keep to these rules, and one draw needn't show every extreme that they name: `roles`: each role id names one adapter.
All inputs are finite; a program needn't handle non-finite values. No bound on the sum of `live` on one device may be relied on, other than what follows from the above.
Results may differ from the reference program's by a relative error of at most 0.0034.
Values may be sent and summed in bfloat16 or wider, within the bound.
No kernel may reach another device: no remote copies, remote signals or barrier semaphores. Data moves between devices by JAX's collectives and lax.ppermute only.
A program may use at most 128 MiB of HBM per device.

```python
import math
import jax
import jax.numpy as jnp
from jax import lax

D = 8192
ROLES = 8
RANK = 64
BLOCK = 128
TOKENS = 8192
BLOCKS = 64


def touch_ends(array, rng, least, high):
    spot = [jax.random.randint(jax.random.fold_in(rng, axis), (), 0, length) for axis, length in enumerate(array.shape)]
    widest = array.shape.index(max(array.shape))
    beside = spot[:widest] + [(spot[widest] + 1) % array.shape[widest]] + spot[widest + 1:]
    return array.at[tuple(spot)].set(least).at[tuple(beside)].set(high)


def level_of(key, shape, shards, least, high):
    gain = 1.0
    for position, parts in shards:
        draws = jax.random.uniform(jax.random.fold_in(jax.random.fold_in(key, 6), position), (parts,), jnp.float32, least / len(shards), high / len(shards))
        gain = gain * jnp.repeat(jnp.exp(draws), shape[position] // parts).reshape((-1,) + (1,) * (len(shape) - 1 - position))
    return gain


def choose_distinct(own_key, rows, amount, top, lift):
    order = jax.random.permutation(jax.random.fold_in(own_key, 1), amount)
    boost = order
    for power in range(3):
        boost = boost * boost // amount
    boost = boost * lift // amount
    chance = jax.random.randint(jax.random.fold_in(own_key, 2), (rows, amount), 0, 4096) + boost
    sure = jax.random.permutation(jax.random.fold_in(own_key, 3), rows)[jnp.arange(amount) % rows]
    chance = jnp.where(jnp.arange(rows)[:, None] == sure[None, :], 1 << 14, chance)
    score = chance * amount + jnp.arange(amount)
    return lax.top_k(score.astype(jnp.int32), top)[1].astype(jnp.int32)


def centred(stream_key, shape, spread, bound, shards=(), kind=jnp.bfloat16):
    factor_of = level_of(stream_key, shape, shards, -0.22, 0.18) if shards else 1.0
    entries = jax.random.normal(stream_key, shape, jnp.float32) * spread * factor_of
    return jnp.minimum(jnp.maximum(entries, -bound), bound).astype(kind)


def setup_inputs(seed: int = 0) -> dict:
    seeds = jax.random.split(jax.random.key(seed), 8)
    attention_output = centred(seeds[0], (TOKENS, D), 1.0, 6.0, ((0, 16), (1, 16)))
    grad_out = centred(seeds[1], (TOKENS, D), 1.0, 6.0, ((0, 16), (1, 16)))
    base_weight = centred(seeds[2], (D, D), D ** -0.5, 0.0625, ((0, 16), (1, 16)))
    adapter_down = centred(seeds[3], (ROLES, D, RANK), D ** -0.5, 0.0625, ((1, 16),))
    adapter_up = centred(seeds[4], (ROLES, RANK, D), D ** -0.5, 0.0625, ((2, 16),))
    roles = choose_distinct(seeds[5], BLOCKS, ROLES, 1, 1024)
    live = touch_ends((jax.random.randint(seeds[6], (BLOCKS,), 0, 4) < 3).astype(jnp.int32), jax.random.fold_in(seeds[6], 1), 0, 1)
    return {"attention_output": attention_output, "grad_out": grad_out, "base_weight": base_weight, "adapter_down": adapter_down, "adapter_up": adapter_up, "roles": roles, "live": live}


adapter_scale = 2.0

def reference(attention_output, grad_out, base_weight, adapter_down, adapter_up, roles, live):
    grad_scale = adapter_scale * math.sqrt(ROLES / TOKENS)
    token_role = jnp.repeat(roles[:, 0], BLOCK)
    token_live = jnp.repeat(live, BLOCK)
    masked_rows = jnp.where(token_live[:, None] > 0, grad_out, jnp.zeros_like(grad_out))
    onehot = (token_role[:, None] == jnp.arange(ROLES, dtype=jnp.int32)[None, :]).astype(jnp.float32)
    flattened_down = jnp.transpose(adapter_down, (1, 0, 2)).reshape(D, ROLES * RANK)
    up_flat = adapter_up.reshape(ROLES * RANK, D)
    low_all = jnp.dot(attention_output, flattened_down, preferred_element_type=jnp.float32).reshape(TOKENS, ROLES, RANK)
    back_all = jnp.dot(masked_rows, up_flat.T, preferred_element_type=jnp.float32).reshape(TOKENS, ROLES, RANK)
    low = lax.optimization_barrier(jnp.sum(onehot[:, :, None] * low_all, axis=1))
    back = lax.optimization_barrier(jnp.sum(onehot[:, :, None] * back_all, axis=1))
    lowrank_wide_rows = (onehot[:, :, None] * low[:, None, :]).reshape(TOKENS, ROLES * RANK).astype(jnp.bfloat16)
    backward_wide_rows = (onehot[:, :, None] * back[:, None, :]).reshape(TOKENS, ROLES * RANK).astype(jnp.bfloat16)
    frozen_base_term = jnp.dot(masked_rows, base_weight.T, preferred_element_type=jnp.float32)
    adapter_term = jnp.dot(backward_wide_rows, flattened_down.T, preferred_element_type=jnp.float32)
    input_gradient = (frozen_base_term + adapter_scale * adapter_term).astype(jnp.bfloat16)
    down_gradient = grad_scale * jnp.dot(attention_output.T, backward_wide_rows, preferred_element_type=jnp.float32)
    down_gradient = jnp.transpose(down_gradient.reshape(D, ROLES, RANK), (1, 0, 2))
    up_gradient = grad_scale * jnp.dot(lowrank_wide_rows.T, masked_rows, preferred_element_type=jnp.float32)
    return (input_gradient, down_gradient, up_gradient.reshape(ROLES, RANK, D))
```

```python
import functools
import math

import jax
import jax.numpy as jnp
from jax import lax
from jax.experimental import pallas as pl
from jax.experimental.pallas import tpu as pltpu
from jax.sharding import Mesh, PartitionSpec as P

adapter_scale = 2.0
Z, XH, XL, Y, C = 8, 2, 2, 4, 2
FS = ("z", "xh")
TP = ("xl", "y", "c")
ROLES = 8
RANK = 64
BLOCK = 128
BLOCKS = 4
GROUP = RANK // Z
ROWS = 512
COLS = 512
PAD = 128
OFFSETS = (0, -1, 1, -2, 2, -3, 3, -4)
f32 = jnp.float32
bf16 = jnp.bfloat16


def dot(a, b, ca, cb):
    return lax.dot_general(a, b, (((ca,), (cb,)), ((), ())), preferred_element_type=f32)


def rank_kernel(roles, att, g, down, up, out):
    out[:, :RANK] = dot(att[...], down[0], 1, 1)
    out[:, RANK:] = dot(g[...], up[0], 1, 1)


def rank_parts(roles, att, g, down, up):
    spec = pltpu.PrefetchScalarGridSpec(
        num_scalar_prefetch=1,
        grid=(BLOCKS,),
        in_specs=[
            pl.BlockSpec((BLOCK, COLS), lambda i, r: (i, 0)),
            pl.BlockSpec((BLOCK, COLS), lambda i, r: (i, 0)),
            pl.BlockSpec((1, RANK, COLS), lambda i, r: (r[i], 0, 0)),
            pl.BlockSpec((1, RANK, COLS), lambda i, r: (r[i], 0, 0)),
        ],
        out_specs=pl.BlockSpec((BLOCK, 2 * RANK), lambda i, r: (i, 0)),
    )
    return pl.pallas_call(
        rank_kernel,
        grid_spec=spec,
        out_shape=jax.ShapeDtypeStruct((ROWS, 2 * RANK), f32),
        cost_estimate=pl.CostEstimate(flops=2 * 2 * ROWS * COLS * RANK, bytes_accessed=2 << 20, transcendentals=0),
    )(roles, att, g, down, up)


def outer_kernel(roles, live, lb, att, g, out):
    for pair in range(BLOCKS // 2):
        ups, downs = [], []
        for b in (2 * pair, 2 * pair + 1):
            rows = pl.ds(b * BLOCK, BLOCK)
            ranks = lb[rows, :]
            ranks = jnp.where(live[b] > 0, ranks, jnp.zeros_like(ranks))
            ups.append(dot(ranks[:, :RANK], g[rows, :], 0, 0))
            downs.append(dot(ranks[:, RANK:], att[rows, :], 0, 0))
        at = pl.ds(2 * GROUP * pair, 2 * GROUP)
        first = lax.broadcasted_iota(jnp.int32, (2 * GROUP, PAD), 0) < GROUP
        ids = jnp.where(first, roles[2 * pair], roles[2 * pair + 1]).astype(f32).astype(bf16)
        for z in range(Z):
            for o, terms in enumerate((ups, downs)):
                part = [t[GROUP * z : GROUP * (z + 1), :] for t in terms]
                out[2 * z + o, at, :COLS] = jnp.concatenate(part, axis=0).astype(bf16)
                out[2 * z + o, at, COLS:] = ids


def outer_parts(roles, live, lb, att, g):
    spec = pltpu.PrefetchScalarGridSpec(
        num_scalar_prefetch=2,
        grid=(1,),
        in_specs=[
            pl.BlockSpec((ROWS, 2 * RANK), lambda i, r, l: (0, 0)),
            pl.BlockSpec((ROWS, COLS), lambda i, r, l: (0, 0)),
            pl.BlockSpec((ROWS, COLS), lambda i, r, l: (0, 0)),
        ],
        out_specs=pl.BlockSpec((Z * XH, BLOCKS * GROUP, COLS + PAD), lambda i, r, l: (0, 0, 0)),
    )
    return pl.pallas_call(
        outer_kernel,
        grid_spec=spec,
        out_shape=jax.ShapeDtypeStruct((Z * XH, BLOCKS * GROUP, COLS + PAD), bf16),
        compiler_params=pltpu.CompilerParams(vmem_limit_bytes=16 << 20),
        cost_estimate=pl.CostEstimate(flops=2 * 2 * ROWS * COLS * RANK, bytes_accessed=2 << 20, transcendentals=0),
    )(roles, live, lb, att, g)


def sum_kernel(scale, recv, out):
    got = recv[...]
    shape = (Z * XH * BLOCKS * GROUP, PAD)
    row = lax.broadcasted_iota(jnp.int32, shape, 0)
    lane = lax.broadcasted_iota(jnp.int32, shape, 1)
    role = got[:, COLS:].astype(f32)
    pick = (role == (lane // GROUP).astype(f32)) & (lane % GROUP == row % GROUP)
    total = dot(pick.astype(f32).astype(bf16), got[:, :COLS], 0, 0)
    total = (scale * total[: ROLES * GROUP, :]).astype(bf16)
    for i in range(Z * XH):
        out[i] = total


def sum_parts(recv, scale):
    rows = Z * XH * BLOCKS * GROUP
    return pl.pallas_call(
        functools.partial(sum_kernel, scale),
        out_shape=jax.ShapeDtypeStruct((Z * XH, ROLES * GROUP, COLS), bf16),
        compiler_params=pltpu.CompilerParams(vmem_limit_bytes=16 << 20),
        cost_estimate=pl.CostEstimate(flops=2 * rows * PAD * COLS, bytes_accessed=2 << 20, transcendentals=0),
    )(recv.reshape(rows, COLS + PAD))


def spread_kernel(recv, up, down):
    for half in range(2):
        ups, downs = [], []
        for z in range(Z):
            ups.append(recv[2 * z].astype(f32)[GROUP * half : GROUP * (half + 1), :])
            downs.append(recv[2 * z + 1].astype(f32)[GROUP * half : GROUP * (half + 1), :])
        up[half] = jnp.concatenate(ups, axis=0)
        down[half] = jnp.concatenate(downs, axis=0)


def spread(recv):
    return pl.pallas_call(
        spread_kernel,
        grid=(ROLES // 2,),
        in_specs=[pl.BlockSpec((Z * XH, 2 * GROUP, COLS), lambda i: (0, i, 0))],
        out_specs=[
            pl.BlockSpec((2, RANK, COLS), lambda i: (i, 0, 0)),
            pl.BlockSpec((2, RANK, COLS), lambda i: (i, 0, 0)),
        ],
        out_shape=[
            jax.ShapeDtypeStruct((ROLES, RANK, COLS), f32),
            jax.ShapeDtypeStruct((ROLES, RANK, COLS), f32),
        ],
        compiler_params=pltpu.CompilerParams(vmem_limit_bytes=16 << 20),
        cost_estimate=pl.CostEstimate(flops=0, bytes_accessed=4 << 20, transcendentals=0),
    )(recv)


def base_sum(place, a, weights):
    total = None
    for off, w in zip(OFFSETS, weights):
        j = lax.rem(place[0] + (off + Z), Z)
        term = dot(a[j, 0], w[...], 1, 1)
        total = term if total is None else total + term
    return total


def partner_kernel(place, a, *rest):
    rest[-1][...] = base_sum(place, a, rest[:Z]).astype(bf16)


def own_kernel(place, roles, live, a, *rest):
    weights, lb, down, out = rest[:Z], rest[Z], rest[Z + 1], rest[Z + 2]
    total = base_sum(place, a, weights)
    for b in range(BLOCKS):
        rows = pl.ds(b * BLOCK, BLOCK)
        term = dot(lb[rows, RANK:], down[roles[b]], 1, 0)
        mine = total[b * BLOCK : (b + 1) * BLOCK, :] + adapter_scale * term
        out[rows, :] = jnp.where(live[b] > 0, mine, jnp.zeros_like(mine))


def partner_part(place, a, weights):
    whole = pl.BlockSpec((COLS, COLS), lambda i, p: (0, 0))
    spec = pltpu.PrefetchScalarGridSpec(
        num_scalar_prefetch=1,
        grid=(1,),
        in_specs=[pl.BlockSpec((Z, 1, ROWS, COLS), lambda i, p: (0, 1 - p[1], 0, 0))] + [whole] * Z,
        out_specs=pl.BlockSpec((ROWS, COLS), lambda i, p: (0, 0)),
    )
    return pl.pallas_call(
        partner_kernel,
        grid_spec=spec,
        out_shape=jax.ShapeDtypeStruct((ROWS, COLS), bf16),
        compiler_params=pltpu.CompilerParams(vmem_limit_bytes=32 << 20),
        cost_estimate=pl.CostEstimate(flops=2 * ROWS * COLS * COLS * Z, bytes_accessed=8 << 20, transcendentals=0),
    )(place, a, *weights)


def own_part(place, roles, live, a, weights, lb, down):
    whole = pl.BlockSpec((COLS, COLS), lambda i, p, r, l: (0, 0))
    spec = pltpu.PrefetchScalarGridSpec(
        num_scalar_prefetch=3,
        grid=(1,),
        in_specs=[pl.BlockSpec((Z, 1, ROWS, COLS), lambda i, p, r, l: (0, p[1], 0, 0))]
        + [whole] * Z
        + [
            pl.BlockSpec((ROWS, 2 * RANK), lambda i, p, r, l: (0, 0)),
            pl.BlockSpec((ROLES, RANK, COLS), lambda i, p, r, l: (0, 0, 0)),
        ],
        out_specs=pl.BlockSpec((ROWS, COLS), lambda i, p, r, l: (0, 0)),
    )
    return pl.pallas_call(
        own_kernel,
        grid_spec=spec,
        out_shape=jax.ShapeDtypeStruct((ROWS, COLS), f32),
        compiler_params=pltpu.CompilerParams(vmem_limit_bytes=40 << 20),
        cost_estimate=pl.CostEstimate(flops=2 * ROWS * COLS * COLS * Z, bytes_accessed=8 << 20, transcendentals=0),
    )(place, roles, live, a, *weights, lb, down)


def along_z(x, step):
    return lax.ppermute(x, "z", [(i, (i + step) % Z) for i in range(Z)])


def shards(attention_output, grad_out, base_weight, adapter_down, adapter_up, roles, live):
    roles = roles[:, 0]
    adapter_down = jnp.transpose(adapter_down, (0, 2, 1))
    tokens = attention_output.shape[0] * Z * XH
    grad_scale = adapter_scale * math.sqrt(ROLES / tokens)
    place = jnp.stack([lax.axis_index("z"), lax.axis_index("xh")]).astype(jnp.int32)

    turned = lax.ppermute(grad_out, ("xh", "c"), [(0, 0), (1, 2), (2, 1), (3, 3)])
    whole = lax.all_gather(turned, TP)

    weights = [base_weight]
    one = two = base_weight
    for step in range(4):
        one = along_z(one, 1)
        weights.append(one)
        if step < 3:
            two = along_z(two, -1)
            weights.append(two)

    parts = rank_parts(roles, attention_output, grad_out, adapter_down, adapter_up)
    parts = lax.all_to_all(parts.reshape(16, ROWS // 16, 2 * RANK), TP, 0, 0)
    mine = jnp.sum(parts, axis=0).astype(bf16)
    lb = lax.all_to_all(jnp.broadcast_to(mine[None], (16,) + mine.shape), TP, 0, 0)
    lb = lb.reshape(ROWS, 2 * RANK)

    outer = outer_parts(roles, live, lb, attention_output, grad_out)
    outer = lax.all_to_all(outer, FS, 0, 0)
    total = sum_parts(outer, grad_scale)
    total = lax.all_to_all(total, FS, 0, 0)
    up_gradient, down_gradient = spread(total)

    a = whole.reshape(Z, XH, ROWS, COLS)
    partner = partner_part(place, a, weights)
    got = lax.ppermute(partner, "xh", [(0, 1), (1, 0)])
    own = own_part(place, roles, live, a, weights, lb, adapter_down)
    token_live = jnp.repeat(live, BLOCK)[:, None] > 0
    input_gradient = jnp.where(token_live, own + got.astype(f32), 0.0).astype(bf16)
    return (input_gradient, jnp.transpose(down_gradient, (0, 2, 1)), up_gradient)


def solution(mesh):
    fine = Mesh(mesh.devices.reshape(Z, XH, XL, Y, C), ("z", "xh", "xl", "y", "c"))
    placed = (
        P(FS, TP),
        P(FS, TP),
        P(TP, FS),
        P(None, TP, None),
        P(None, None, TP),
        P(FS, None),
        P(FS),
    )
    return jax.shard_map(
        shards,
        mesh=fine,
        in_specs=placed,
        out_specs=(P(FS, TP), P(None, TP, None), P(None, None, TP)),
        check_vma=False,
    )
```

```python
import functools
import math

import jax
import jax.numpy as jnp
from jax import lax
from jax.experimental import pallas as pl
from jax.experimental.pallas import tpu as pltpu
from jax.sharding import Mesh, PartitionSpec as P

adapter_scale = 2.0
Z, XH, XL, Y, C = 8, 2, 2, 4, 2
FS = ("z", "xh")
TP = ("xl", "y", "c")
ROLES = 8
RANK = 64
BLOCK = 128
BLOCKS = 4
GROUP = RANK // Z
ROWS = 512
COLS = 512
PAD = 128
VMEM = 24 << 20
FULL = 56 << 20
OFFSETS = (0, -1, 1, -2, 2, -3, 3, -4)
MOST = 50 << 20
TILE = 256
f32 = jnp.float32
bf16 = jnp.bfloat16


def dot(a, b, ca, cb):
    return lax.dot_general(a, b, (((ca,), (cb,)), ((), ())), preferred_element_type=f32)


def rank_kernel(roles, att, g, down, up, out):
    for b in range(BLOCKS):
        rows = pl.ds(b * BLOCK, BLOCK)
        out[rows, :RANK] = dot(att[rows, :], down[roles[b]], 1, 1)
        out[rows, RANK:] = dot(g[rows, :], up[roles[b]], 1, 1)


def whole(shape):
    return pl.BlockSpec(shape, lambda i, p: (0,) * len(shape))


def rank_parts(roles, att, g, down, up):
    spec = pltpu.PrefetchScalarGridSpec(
        num_scalar_prefetch=1,
        grid=(1,),
        in_specs=[
            whole((ROWS, COLS)),
            whole((ROWS, COLS)),
            whole((ROLES, RANK, COLS)),
            whole((ROLES, RANK, COLS)),
        ],
        out_specs=whole((ROWS, 2 * RANK)),
    )
    return pl.pallas_call(
        rank_kernel,
        grid_spec=spec,
        out_shape=jax.ShapeDtypeStruct((ROWS, 2 * RANK), f32),
        compiler_params=pltpu.CompilerParams(vmem_limit_bytes=FULL),
        cost_estimate=pl.CostEstimate(flops=2 * 2 * ROWS * COLS * RANK, bytes_accessed=2 << 20, transcendentals=0),
    )(roles, att, g, down, up)


def outer_kernel(roles, live, lb, att_far, g_far, out, att, g, sems):
    copies = []
    for b in range(BLOCKS):
        rows = pl.ds(b * BLOCK, BLOCK)
        pairs = ((g_far.at[rows], g.at[rows]), (att_far.at[rows], att.at[rows]))
        copies.append([pltpu.make_async_copy(x, y, sems.at[b, i]) for i, (x, y) in enumerate(pairs)])
        for copy in copies[b]:
            copy.start()
    for pair in range(BLOCKS // 2):
        ups, downs = [], []
        for b in (2 * pair, 2 * pair + 1):
            rows = pl.ds(b * BLOCK, BLOCK)
            for copy in copies[b]:
                copy.wait()
            ranks = lb[rows, :]
            ranks = jnp.where(live[b] > 0, ranks, jnp.zeros_like(ranks))
            ups.append(dot(ranks[:, :RANK], g[rows, :], 0, 0))
            downs.append(dot(ranks[:, RANK:], att[rows, :], 0, 0))
        at = pl.ds(2 * GROUP * pair, 2 * GROUP)
        first = lax.broadcasted_iota(jnp.int32, (2 * GROUP, PAD), 0) < GROUP
        ids = jnp.where(first, roles[2 * pair], roles[2 * pair + 1])
        ids = ids.astype(f32).astype(bf16)
        for z in range(Z):
            for o, terms in enumerate((ups, downs)):
                part = [t[GROUP * z : GROUP * (z + 1), :] for t in terms]
                out[2 * z + o, at, :COLS] = jnp.concatenate(part, axis=0).astype(bf16)
                out[2 * z + o, at, COLS:] = ids


def outer_parts(roles, live, lb, att, g):
    return pl.pallas_call(
        outer_kernel,
        in_specs=[pl.BlockSpec(memory_space=pltpu.SMEM)] * 2
        + [pl.BlockSpec(memory_space=pltpu.VMEM)]
        + [pl.BlockSpec(memory_space=pl.ANY)] * 2,
        out_specs=pl.BlockSpec(memory_space=pltpu.VMEM),
        scratch_shapes=[
            pltpu.VMEM((ROWS, COLS), bf16),
            pltpu.VMEM((ROWS, COLS), bf16),
            pltpu.SemaphoreType.DMA((BLOCKS, 2)),
        ],
        out_shape=jax.ShapeDtypeStruct((Z * XH, BLOCKS * GROUP, COLS + PAD), bf16),
        compiler_params=pltpu.CompilerParams(vmem_limit_bytes=FULL),
        cost_estimate=pl.CostEstimate(flops=2 * 2 * ROWS * COLS * RANK, bytes_accessed=2 << 20, transcendentals=0),
    )(roles, live, lb, att, g)


def sum_kernel(scale, recv, out):
    got = recv[...]
    shape = (Z * XH * BLOCKS * GROUP, PAD)
    row = lax.broadcasted_iota(jnp.int32, shape, 0)
    lane = lax.broadcasted_iota(jnp.int32, shape, 1)
    role = got[:, COLS:].astype(f32)
    pick = (role == (lane // GROUP).astype(f32)) & (lane % GROUP == row % GROUP)
    total = dot(pick.astype(f32).astype(bf16), got[:, :COLS], 0, 0)
    total = (scale * total[: ROLES * GROUP, :]).astype(bf16)
    for i in range(Z * XH):
        out[i] = total


def sum_parts(recv, scale):
    rows = Z * XH * BLOCKS * GROUP
    return pl.pallas_call(
        functools.partial(sum_kernel, scale),
        out_shape=jax.ShapeDtypeStruct((Z * XH, ROLES * GROUP, COLS), bf16),
        compiler_params=pltpu.CompilerParams(vmem_limit_bytes=16 << 20),
        cost_estimate=pl.CostEstimate(flops=2 * rows * PAD * COLS, bytes_accessed=2 << 20, transcendentals=0),
    )(recv.reshape(rows, COLS + PAD))


def spread_kernel(recv, up, down):
    for half in range(2):
        ups, downs = [], []
        for z in range(Z):
            ups.append(recv[2 * z].astype(f32)[GROUP * half : GROUP * (half + 1), :])
            downs.append(recv[2 * z + 1].astype(f32)[GROUP * half : GROUP * (half + 1), :])
        up[half] = jnp.concatenate(ups, axis=0)
        down[half] = jnp.concatenate(downs, axis=0)


def spread(recv):
    return pl.pallas_call(
        spread_kernel,
        grid=(ROLES // 2,),
        in_specs=[pl.BlockSpec((Z * XH, 2 * GROUP, COLS), lambda i: (0, i, 0))],
        out_specs=[pl.BlockSpec((2, RANK, COLS), lambda i: (i, 0, 0))] * 2,
        out_shape=[jax.ShapeDtypeStruct((ROLES, RANK, COLS), f32)] * 2,
        compiler_params=pltpu.CompilerParams(vmem_limit_bytes=VMEM),
        cost_estimate=pl.CostEstimate(flops=0, bytes_accessed=4 << 20, transcendentals=0),
    )(recv)


def base_kernel(place, roles, live, wide, *refs):
    pieces, (lb, down), (far, near, own), (sheets, total, sems) = refs[:8], refs[8:10], refs[10:13], refs[13:]
    x_hi, x_lo, y, core = place[1], place[2], place[3], place[4]
    columns = (x_lo, 1 - x_lo, x_lo, x_lo, 1 - x_lo, 1 - x_lo, x_lo, 1 - x_lo)
    steps = (0, 0, -1, 1, -1, 1, 2, 2)
    blocks = [(p, column, y + Y + step) for p, column, step in zip(pieces, columns, steps)]
    copies = []
    for s, (_, column, row) in enumerate(blocks):
        j = column * Y + lax.rem(row, Y)
        copies.append(pltpu.make_async_copy(wide.at[j], sheets.at[s], sems.at[s]))
        copies[s].start()
    for s, (block, _, _) in enumerate(blocks):
        copies[s].wait()
        for half in range(C):
            term = dot(block[...], sheets[s, half], 1, 1)
            total[half] = term if s == 0 else total[half] + term

    mine = core == x_hi
    far[...] = total[1 - core].astype(bf16)
    near[...] = total[jnp.where(mine, 1 - core, core)].astype(bf16)
    for b in range(BLOCKS):
        rows = pl.ds(b * BLOCK, BLOCK)
        term = adapter_scale * dot(lb[rows, RANK:], down[roles[b]], 1, 0)
        part = total[core, rows, :]
        part = jnp.where(mine, part, jnp.zeros_like(part)) + term
        own[rows, :] = jnp.where(live[b] > 0, part, jnp.zeros_like(part))


def base_parts(place, roles, live, wide, *pieces):
    here = pl.BlockSpec(memory_space=pltpu.VMEM)
    return pl.pallas_call(
        base_kernel,
        in_specs=[pl.BlockSpec(memory_space=pltpu.SMEM)] * 3
        + [pl.BlockSpec(memory_space=pl.ANY)]
        + [here] * len(pieces),
        out_specs=[here] * 3,
        scratch_shapes=[
            pltpu.VMEM((Z, C, COLS, COLS), bf16),
            pltpu.VMEM((C, ROWS, COLS), f32),
            pltpu.SemaphoreType.DMA((Z,)),
        ],
        out_shape=[
            jax.ShapeDtypeStruct((ROWS, COLS), bf16),
            jax.ShapeDtypeStruct((ROWS, COLS), bf16),
            jax.ShapeDtypeStruct((ROWS, COLS), f32),
        ],
        compiler_params=pltpu.CompilerParams(vmem_limit_bytes=MOST),
        cost_estimate=pl.CostEstimate(flops=4 * ROWS * COLS * COLS * Z, bytes_accessed=14 << 20, transcendentals=0),
    )(place, roles, live, wide, *pieces)


def shift(x, axis, size, step):
    return lax.ppermute(x, axis, [(i, (i + step) % size) for i in range(size)])


def tie(*values):
    return lax.optimization_barrier(values)


def trade(x, axis, size, bit):
    return lax.ppermute(x, axis, [(i, i ^ bit) for i in range(size)])


def shards(attention_output, grad_out, base_weight, adapter_down, adapter_up, roles, live):
    adapter_down = jnp.transpose(adapter_down, (0, 2, 1))
    tokens = attention_output.shape[0] * Z * XH
    grad_scale = adapter_scale * math.sqrt(ROLES / tokens)
    roles = roles[:, 0]
    place = jnp.stack([lax.axis_index(name) for name in ("z", "xh", "xl", "y", "c")]).astype(jnp.int32)

    wide = lax.all_gather(base_weight, ("z", "c")).reshape(Z, C, COLS, COLS)
    turned = lax.ppermute(grad_out, ("xh", "c"), [(0, 0), (1, 2), (2, 1), (3, 3)])
    ranks = rank_parts(roles, attention_output, grad_out, adapter_down, adapter_up)
    ranks = lax.all_to_all(ranks.reshape(16, ROWS // 16, 2 * RANK), TP, 0, 0)
    ranks, turned = tie(ranks, turned)

    beside = trade(turned, "xl", XL, 1)
    up1, down1 = shift(turned, "y", Y, 1), shift(turned, "y", Y, -1)
    mine = jnp.sum(ranks, axis=0).astype(bf16)
    lb = lax.all_to_all(jnp.broadcast_to(mine[None], (16,) + mine.shape), TP, 0, 0)
    lb, beside, up1, down1 = tie(lb.reshape(ROWS, 2 * RANK), beside, up1, down1)

    up2, beside_down1 = shift(up1, "y", Y, 1), shift(beside, "y", Y, -1)
    outer = outer_parts(roles, live, lb, attention_output, grad_out)
    outer = lax.all_to_all(outer, FS, 0, 0)
    beside_up1, beside_down2 = shift(beside, "y", Y, 1), shift(beside_down1, "y", Y, -1)
    outer, up2, beside_up1, beside_down2 = tie(outer, up2, beside_up1, beside_down2)
    pieces = [turned, beside, up1, down1, beside_up1, beside_down1, up2, beside_down2]

    total = lax.all_to_all(sum_parts(outer, grad_scale), FS, 0, 0)
    far, near, own = base_parts(place, roles, live, wide, *pieces, lb, adapter_down)
    far = lax.ppermute(far, ("xh", "c"), [(1, 2), (2, 1)])
    near = lax.ppermute(near, ("xh", "c"), [(0, 1), (1, 3), (2, 0), (3, 2)])
    total, own = tie(total, own)
    up_gradient, down_gradient = spread(total)
    token_live = jnp.repeat(live, BLOCK)[:, None] > 0
    input_gradient = jnp.where(token_live, own + far.astype(f32) + near.astype(f32), 0.0).astype(bf16)
    return (input_gradient, jnp.transpose(down_gradient, (0, 2, 1)), up_gradient)


def solution(mesh):
    fine = Mesh(mesh.devices.reshape(Z, XH, XL, Y, C), ("z", "xh", "xl", "y", "c"))
    placed = (
        P(FS, TP),
        P(FS, TP),
        P(TP, FS),
        P(None, TP, None),
        P(None, None, TP),
        P(FS, None),
        P(FS),
    )
    return jax.shard_map(
        shards,
        mesh=fine,
        in_specs=placed,
        out_specs=(P(FS, TP), P(None, TP, None), P(None, None, TP)),
        check_vma=False,
    )
```

```python
import functools
import math

import jax
import jax.numpy as jnp
from jax import lax
from jax.experimental import pallas as pl
from jax.experimental.pallas import tpu as pltpu
from jax.sharding import Mesh, PartitionSpec as P

adapter_scale = 2.0
Z, XH, XL, Y, C = 8, 2, 2, 4, 2
FS = ("z", "xh")
TP = ("xl", "y", "c")
ROLES = 8
RANK = 64
BLOCK = 128
BLOCKS = 4
GROUP = RANK // Z
ROWS = 512
COLS = 512
PAD = 128
VMEM = 24 << 20
FULL = 56 << 20
OFFSETS = (0, -1, 1, -2, 2, -3, 3, -4)
MOST = 50 << 20
TILE = 256
f32 = jnp.float32
bf16 = jnp.bfloat16


def dot(a, b, ca, cb):
    return lax.dot_general(a, b, (((ca,), (cb,)), ((), ())), preferred_element_type=f32)


def rank_kernel(roles, att, g, down, up, out):
    for b in range(BLOCKS):
        rows = pl.ds(b * BLOCK, BLOCK)
        out[rows, :RANK] = dot(att[rows, :], down[roles[b]], 1, 1)
        out[rows, RANK:] = dot(g[rows, :], up[roles[b]], 1, 1)


def whole(shape):
    return pl.BlockSpec(shape, lambda i, p: (0,) * len(shape))


def rank_parts(roles, att, g, down, up):
    spec = pltpu.PrefetchScalarGridSpec(
        num_scalar_prefetch=1,
        grid=(1,),
        in_specs=[
            whole((ROWS, COLS)),
            whole((ROWS, COLS)),
            whole((ROLES, RANK, COLS)),
            whole((ROLES, RANK, COLS)),
        ],
        out_specs=whole((ROWS, 2 * RANK)),
    )
    return pl.pallas_call(
        rank_kernel,
        grid_spec=spec,
        out_shape=jax.ShapeDtypeStruct((ROWS, 2 * RANK), f32),
        compiler_params=pltpu.CompilerParams(vmem_limit_bytes=FULL),
        cost_estimate=pl.CostEstimate(flops=2 * 2 * ROWS * COLS * RANK, bytes_accessed=2 << 20, transcendentals=0),
    )(roles, att, g, down, up)


def outer_kernel(roles, live, lb, att_far, g_far, out, att, g, sems):
    copies = []
    for b in range(BLOCKS):
        rows = pl.ds(b * BLOCK, BLOCK)
        pairs = ((g_far.at[rows], g.at[rows]), (att_far.at[rows], att.at[rows]))
        copies.append([pltpu.make_async_copy(x, y, sems.at[b, i]) for i, (x, y) in enumerate(pairs)])
        for copy in copies[b]:
            copy.start()
    for pair in range(BLOCKS // 2):
        ups, downs = [], []
        for b in (2 * pair, 2 * pair + 1):
            rows = pl.ds(b * BLOCK, BLOCK)
            for copy in copies[b]:
                copy.wait()
            ranks = lb[rows, :]
            ranks = jnp.where(live[b] > 0, ranks, jnp.zeros_like(ranks))
            ups.append(dot(ranks[:, :RANK], g[rows, :], 0, 0))
            downs.append(dot(ranks[:, RANK:], att[rows, :], 0, 0))
        at = pl.ds(2 * GROUP * pair, 2 * GROUP)
        first = lax.broadcasted_iota(jnp.int32, (2 * GROUP, PAD), 0) < GROUP
        ids = jnp.where(first, roles[2 * pair], roles[2 * pair + 1])
        ids = ids.astype(f32).astype(bf16)
        for z in range(Z):
            for o, terms in enumerate((ups, downs)):
                part = [t[GROUP * z : GROUP * (z + 1), :] for t in terms]
                out[2 * z + o, at, :COLS] = jnp.concatenate(part, axis=0).astype(bf16)
                out[2 * z + o, at, COLS:] = ids


def outer_parts(roles, live, lb, att, g):
    return pl.pallas_call(
        outer_kernel,
        in_specs=[pl.BlockSpec(memory_space=pltpu.SMEM)] * 2
        + [pl.BlockSpec(memory_space=pltpu.VMEM)]
        + [pl.BlockSpec(memory_space=pl.ANY)] * 2,
        out_specs=pl.BlockSpec(memory_space=pltpu.VMEM),
        scratch_shapes=[
            pltpu.VMEM((ROWS, COLS), bf16),
            pltpu.VMEM((ROWS, COLS), bf16),
            pltpu.SemaphoreType.DMA((BLOCKS, 2)),
        ],
        out_shape=jax.ShapeDtypeStruct((Z * XH, BLOCKS * GROUP, COLS + PAD), bf16),
        compiler_params=pltpu.CompilerParams(vmem_limit_bytes=FULL),
        cost_estimate=pl.CostEstimate(flops=2 * 2 * ROWS * COLS * RANK, bytes_accessed=2 << 20, transcendentals=0),
    )(roles, live, lb, att, g)


def sum_kernel(scale, recv, out):
    got = recv[...]
    shape = (Z * XH * BLOCKS * GROUP, PAD)
    row = lax.broadcasted_iota(jnp.int32, shape, 0)
    lane = lax.broadcasted_iota(jnp.int32, shape, 1)
    role = got[:, COLS:].astype(f32)
    pick = (role == (lane // GROUP).astype(f32)) & (lane % GROUP == row % GROUP)
    total = dot(pick.astype(f32).astype(bf16), got[:, :COLS], 0, 0)
    out[...] = (scale * total[: ROLES * GROUP, :]).astype(bf16)


def sum_parts(recv, scale):
    rows = Z * XH * BLOCKS * GROUP
    return pl.pallas_call(
        functools.partial(sum_kernel, scale),
        out_shape=jax.ShapeDtypeStruct((ROLES * GROUP, COLS), bf16),
        compiler_params=pltpu.CompilerParams(vmem_limit_bytes=16 << 20),
        cost_estimate=pl.CostEstimate(flops=2 * rows * PAD * COLS, bytes_accessed=2 << 20, transcendentals=0),
    )(recv.reshape(rows, COLS + PAD))


def spread_kernel(place, *refs):
    pieces, up, down = refs[:Z], refs[Z], refs[Z + 1]
    for off, piece in zip(OFFSETS, pieces):
        z = lax.rem(place[0] + (off + Z), Z)
        at = pl.ds(pl.multiple_of(GROUP * z, GROUP), GROUP)
        for o, out in enumerate((up, down)):
            rows = piece[o].astype(f32)
            for k in range(ROLES):
                out[k, at, :] = rows[GROUP * k : GROUP * (k + 1), :]


def spread(place, pieces):
    spec = pltpu.PrefetchScalarGridSpec(
        num_scalar_prefetch=1,
        grid=(1,),
        in_specs=[whole((2, ROLES * GROUP, COLS))] * Z,
        out_specs=[whole((ROLES, RANK, COLS))] * 2,
    )
    return pl.pallas_call(
        spread_kernel,
        grid_spec=spec,
        out_shape=[jax.ShapeDtypeStruct((ROLES, RANK, COLS), f32)] * 2,
        compiler_params=pltpu.CompilerParams(vmem_limit_bytes=VMEM),
        cost_estimate=pl.CostEstimate(flops=0, bytes_accessed=4 << 20, transcendentals=0),
    )(place, *pieces)


def base_kernel(place, roles, live, wide, *refs):
    pieces, (lb_far, down_far), (far, near, own) = refs[:Z], refs[Z : Z + 2], refs[Z + 2 : Z + 5]
    held, sheets, total, lb, down, sems = refs[Z + 5 :]
    x_hi, x_lo, y, core = place[1], place[2], place[3], place[4]
    columns = (x_lo, 1 - x_lo, x_lo, x_lo, 1 - x_lo, 1 - x_lo, x_lo, 1 - x_lo)
    steps = (0, 0, -1, 1, -1, 1, 2, 2)
    copies = []
    for s, (piece, column, step) in enumerate(zip(pieces, columns, steps)):
        j = column * Y + lax.rem(y + Y + step, Y)
        copies.append(
            (
                pltpu.make_async_copy(piece, held.at[s], sems.at[s, 0]),
                pltpu.make_async_copy(wide.at[j], sheets.at[s], sems.at[s, 1]),
            )
        )
    copies.append(
        (
            pltpu.make_async_copy(lb_far, lb, sems.at[Z, 0]),
            pltpu.make_async_copy(down_far, down, sems.at[Z, 1]),
        )
    )
    for pair in copies:
        for copy in pair:
            copy.start()
    for s in range(Z):
        for copy in copies[s]:
            copy.wait()
        for half in range(C):
            term = dot(held[s], sheets[s, half], 1, 1)
            total[half] = term if s == 0 else total[half] + term
    for copy in copies[Z]:
        copy.wait()

    mine = core == x_hi
    far[...] = total[1 - core].astype(bf16)
    near[...] = total[jnp.where(mine, 1 - core, core)].astype(bf16)
    for b in range(BLOCKS):
        rows = pl.ds(b * BLOCK, BLOCK)
        term = adapter_scale * dot(lb[rows, RANK:], down[roles[b]], 1, 0)
        part = total[core, rows, :]
        part = jnp.where(mine, part, jnp.zeros_like(part)) + term
        own[rows, :] = jnp.where(live[b] > 0, part, jnp.zeros_like(part))


def base_parts(place, roles, live, wide, *pieces):
    spec = pltpu.PrefetchScalarGridSpec(
        num_scalar_prefetch=3,
        grid=(1,),
        in_specs=[pl.BlockSpec(memory_space=pl.ANY)] * (1 + len(pieces)),
        out_specs=[pl.BlockSpec((ROWS, COLS), lambda i, p, r, l: (0, 0))] * 3,
        scratch_shapes=[
            pltpu.VMEM((Z, ROWS, COLS), bf16),
            pltpu.VMEM((Z, C, COLS, COLS), bf16),
            pltpu.VMEM((C, ROWS, COLS), f32),
            pltpu.VMEM((ROWS, 2 * RANK), bf16),
            pltpu.VMEM((ROLES, RANK, COLS), bf16),
            pltpu.SemaphoreType.DMA((Z + 1, 2)),
        ],
    )
    return pl.pallas_call(
        base_kernel,
        grid_spec=spec,
        out_shape=[
            jax.ShapeDtypeStruct((ROWS, COLS), bf16),
            jax.ShapeDtypeStruct((ROWS, COLS), bf16),
            jax.ShapeDtypeStruct((ROWS, COLS), f32),
        ],
        compiler_params=pltpu.CompilerParams(vmem_limit_bytes=MOST),
        cost_estimate=pl.CostEstimate(flops=4 * ROWS * COLS * COLS * Z, bytes_accessed=14 << 20, transcendentals=0),
    )(place, roles, live, wide, *pieces)


def shift(x, axis, size, step):
    return lax.ppermute(x, axis, [(i, (i + step) % size) for i in range(size)])


def tie(*values):
    return lax.optimization_barrier(values)


def trade(x, axis, size, bit):
    return lax.ppermute(x, axis, [(i, i ^ bit) for i in range(size)])


def shards(attention_output, grad_out, base_weight, adapter_down, adapter_up, roles, live):
    adapter_down = jnp.transpose(adapter_down, (0, 2, 1))
    tokens = attention_output.shape[0] * Z * XH
    grad_scale = adapter_scale * math.sqrt(ROLES / tokens)
    roles = roles[:, 0]
    place = jnp.stack([lax.axis_index(name) for name in ("z", "xh", "xl", "y", "c")]).astype(jnp.int32)

    wide = lax.all_gather(base_weight, ("z", "c")).reshape(Z, C, COLS, COLS)
    turned = lax.ppermute(grad_out, ("xh", "c"), [(0, 0), (1, 2), (2, 1), (3, 3)])
    ranks = rank_parts(roles, attention_output, grad_out, adapter_down, adapter_up)
    ranks = lax.all_to_all(ranks.reshape(16, ROWS // 16, 2 * RANK), TP, 0, 0)
    ranks, turned = tie(ranks, turned)

    beside = trade(turned, "xl", XL, 1)
    up1, down1 = shift(turned, "y", Y, 1), shift(turned, "y", Y, -1)
    mine = jnp.sum(ranks, axis=0).astype(bf16)
    lb = lax.all_to_all(jnp.broadcast_to(mine[None], (16,) + mine.shape), TP, 0, 0)
    lb, beside, up1, down1 = tie(lb.reshape(ROWS, 2 * RANK), beside, up1, down1)

    up2, beside_down1 = shift(up1, "y", Y, 1), shift(beside, "y", Y, -1)
    outer = outer_parts(roles, live, lb, attention_output, grad_out)
    up2, beside_down1, beside, _ = tie(up2, beside_down1, beside, outer)
    outer = lax.all_to_all(outer, FS, 0, 0)
    beside_up1, beside_down2 = shift(beside, "y", Y, 1), shift(beside_down1, "y", Y, -1)
    pieces = [turned, beside, up1, down1, beside_up1, beside_down1, up2, beside_down2]

    total = sum_parts(outer, grad_scale)
    other = trade(total, "xh", XH, 1)
    far, near, own = base_parts(place, roles, live, wide, *pieces, lb, adapter_down)
    total, other, far, near, own = tie(total, other, far, near, own)

    far = lax.ppermute(far, ("xh", "c"), [(1, 2), (2, 1)])
    near = lax.ppermute(near, ("xh", "c"), [(0, 1), (1, 3), (2, 0), (3, 2)])
    pair = jnp.where(place[1] == 0, jnp.stack([total, other]), jnp.stack([other, total]))
    s1, t1 = shift(pair, "z", Z, 1), shift(pair, "z", Z, -1)
    s2, t2 = shift(pair, "z", Z, 2), shift(pair, "z", Z, -2)
    s3, t3 = shift(s2, "z", Z, 1), shift(t2, "z", Z, -1)
    s4 = shift(s2, "z", Z, 2)
    token_live = jnp.repeat(live, BLOCK)[:, None] > 0
    input_gradient = jnp.where(token_live, own + far.astype(f32) + near.astype(f32), 0.0).astype(bf16)
    input_gradient, s3, t3, s4 = tie(input_gradient, s3, t3, s4)
    up_gradient, down_gradient = spread(place, [pair, s1, t1, s2, t2, s3, t3, s4])
    return (input_gradient, jnp.transpose(down_gradient, (0, 2, 1)), up_gradient)


def solution(mesh):
    fine = Mesh(mesh.devices.reshape(Z, XH, XL, Y, C), ("z", "xh", "xl", "y", "c"))
    placed = (
        P(FS, TP),
        P(FS, TP),
        P(TP, FS),
        P(None, TP, None),
        P(None, None, TP),
        P(FS, None),
        P(FS),
    )
    return jax.shard_map(
        shards,
        mesh=fine,
        in_specs=placed,
        out_specs=(P(FS, TP), P(None, TP, None), P(None, None, TP)),
        check_vma=False,
    )
```

```python
import functools
import math

import jax
import jax.numpy as jnp
from jax import lax
from jax.experimental import pallas as pl
from jax.experimental.pallas import tpu as pltpu
from jax.sharding import Mesh, PartitionSpec as P

adapter_scale = 2.0
Z, XH, XL, Y, C = 8, 2, 2, 4, 2
FS = ("z", "xh")
TP = ("xl", "y", "c")
ROLES = 8
RANK = 64
BLOCK = 128
BLOCKS = 4
GROUP = RANK // Z
ROWS = 512
COLS = 512
PAD = 128
VMEM = 24 << 20
FULL = 56 << 20
OFFSETS = (0, -1, 1, -2, 2, -3, 3, -4)
MOST = 50 << 20
TILE = 256
f32 = jnp.float32
bf16 = jnp.bfloat16


def dot(a, b, ca, cb):
    return lax.dot_general(a, b, (((ca,), (cb,)), ((), ())), preferred_element_type=f32)


def rank_kernel(roles, att, g, down, up, out):
    for b in range(BLOCKS):
        rows = pl.ds(b * BLOCK, BLOCK)
        out[rows, :RANK] = dot(att[rows, :], down[roles[b]], 1, 1)
        out[rows, RANK:] = dot(g[rows, :], up[roles[b]], 1, 1)


def whole(shape):
    return pl.BlockSpec(shape, lambda i, p: (0,) * len(shape))


def rank_parts(roles, att, g, down, up):
    spec = pltpu.PrefetchScalarGridSpec(
        num_scalar_prefetch=1,
        grid=(1,),
        in_specs=[
            whole((ROWS, COLS)),
            whole((ROWS, COLS)),
            whole((ROLES, RANK, COLS)),
            whole((ROLES, RANK, COLS)),
        ],
        out_specs=whole((ROWS, 2 * RANK)),
    )
    return pl.pallas_call(
        rank_kernel,
        grid_spec=spec,
        out_shape=jax.ShapeDtypeStruct((ROWS, 2 * RANK), f32),
        compiler_params=pltpu.CompilerParams(vmem_limit_bytes=FULL),
        cost_estimate=pl.CostEstimate(flops=2 * 2 * ROWS * COLS * RANK, bytes_accessed=2 << 20, transcendentals=0),
    )(roles, att, g, down, up)


def outer_kernel(roles, live, lb, att_far, g_far, out, att, g, sems):
    copies = []
    for b in range(BLOCKS):
        rows = pl.ds(b * BLOCK, BLOCK)
        pairs = ((g_far.at[rows], g.at[rows]), (att_far.at[rows], att.at[rows]))
        copies.append([pltpu.make_async_copy(x, y, sems.at[b, i]) for i, (x, y) in enumerate(pairs)])
        for copy in copies[b]:
            copy.start()
    for pair in range(BLOCKS // 2):
        ups, downs = [], []
        for b in (2 * pair, 2 * pair + 1):
            rows = pl.ds(b * BLOCK, BLOCK)
            for copy in copies[b]:
                copy.wait()
            ranks = lb[rows, :]
            ranks = jnp.where(live[b] > 0, ranks, jnp.zeros_like(ranks))
            ups.append(dot(ranks[:, :RANK], g[rows, :], 0, 0))
            downs.append(dot(ranks[:, RANK:], att[rows, :], 0, 0))
        at = pl.ds(2 * GROUP * pair, 2 * GROUP)
        first = lax.broadcasted_iota(jnp.int32, (2 * GROUP, PAD), 0) < GROUP
        ids = jnp.where(first, roles[2 * pair], roles[2 * pair + 1])
        ids = ids.astype(f32).astype(bf16)
        for z in range(Z):
            for o, terms in enumerate((ups, downs)):
                part = [t[GROUP * z : GROUP * (z + 1), :] for t in terms]
                out[2 * z + o, at, :COLS] = jnp.concatenate(part, axis=0).astype(bf16)
                out[2 * z + o, at, COLS:] = ids


def outer_parts(roles, live, lb, att, g):
    return pl.pallas_call(
        outer_kernel,
        in_specs=[pl.BlockSpec(memory_space=pltpu.SMEM)] * 2
        + [pl.BlockSpec(memory_space=pltpu.VMEM)]
        + [pl.BlockSpec(memory_space=pl.ANY)] * 2,
        out_specs=pl.BlockSpec(memory_space=pltpu.VMEM),
        scratch_shapes=[
            pltpu.VMEM((ROWS, COLS), bf16),
            pltpu.VMEM((ROWS, COLS), bf16),
            pltpu.SemaphoreType.DMA((BLOCKS, 2)),
        ],
        out_shape=jax.ShapeDtypeStruct((Z * XH, BLOCKS * GROUP, COLS + PAD), bf16),
        compiler_params=pltpu.CompilerParams(vmem_limit_bytes=FULL),
        cost_estimate=pl.CostEstimate(flops=2 * 2 * ROWS * COLS * RANK, bytes_accessed=2 << 20, transcendentals=0),
    )(roles, live, lb, att, g)


def sum_kernel(scale, recv, out):
    got = recv[...]
    shape = (Z * XH * BLOCKS * GROUP, PAD)
    row = lax.broadcasted_iota(jnp.int32, shape, 0)
    lane = lax.broadcasted_iota(jnp.int32, shape, 1)
    role = got[:, COLS:].astype(f32)
    pick = (role == (lane // GROUP).astype(f32)) & (lane % GROUP == row % GROUP)
    total = dot(pick.astype(f32).astype(bf16), got[:, :COLS], 0, 0)
    out[...] = (scale * total[: ROLES * GROUP, :]).astype(bf16)


def sum_parts(recv, scale):
    rows = Z * XH * BLOCKS * GROUP
    return pl.pallas_call(
        functools.partial(sum_kernel, scale),
        out_shape=jax.ShapeDtypeStruct((ROLES * GROUP, COLS), bf16),
        compiler_params=pltpu.CompilerParams(vmem_limit_bytes=16 << 20),
        cost_estimate=pl.CostEstimate(flops=2 * rows * PAD * COLS, bytes_accessed=2 << 20, transcendentals=0),
    )(recv.reshape(rows, COLS + PAD))


def spread_kernel(place, *refs):
    pieces, up, down = refs[:Z], refs[Z], refs[Z + 1]
    for off, piece in zip(OFFSETS, pieces):
        z = lax.rem(place[0] + (off + Z), Z)
        at = pl.ds(pl.multiple_of(GROUP * z, GROUP), GROUP)
        for o, out in enumerate((up, down)):
            rows = piece[o].astype(f32)
            for k in range(ROLES):
                out[k, at, :] = rows[GROUP * k : GROUP * (k + 1), :]


def spread(place, pieces):
    spec = pltpu.PrefetchScalarGridSpec(
        num_scalar_prefetch=1,
        grid=(1,),
        in_specs=[whole((2, ROLES * GROUP, COLS))] * Z,
        out_specs=[whole((ROLES, RANK, COLS))] * 2,
    )
    return pl.pallas_call(
        spread_kernel,
        grid_spec=spec,
        out_shape=[jax.ShapeDtypeStruct((ROLES, RANK, COLS), f32)] * 2,
        compiler_params=pltpu.CompilerParams(vmem_limit_bytes=VMEM),
        cost_estimate=pl.CostEstimate(flops=0, bytes_accessed=4 << 20, transcendentals=0),
    )(place, *pieces)


def base_kernel(place, roles, live, wide, *refs):
    pieces, (lb_far, down_far), (far, near, own) = refs[:Z], refs[Z : Z + 2], refs[Z + 2 : Z + 5]
    held, sheets, total, lb, down, sems = refs[Z + 5 :]
    x_hi, x_lo, y, core = place[1], place[2], place[3], place[4]
    columns = (x_lo, 1 - x_lo, x_lo, x_lo, 1 - x_lo, 1 - x_lo, x_lo, 1 - x_lo)
    steps = (0, 0, -1, 1, -1, 1, 2, 2)
    copies = []
    for s, (piece, column, step) in enumerate(zip(pieces, columns, steps)):
        j = column * Y + lax.rem(y + Y + step, Y)
        copies.append(
            (
                pltpu.make_async_copy(piece, held.at[s], sems.at[s, 0]),
                pltpu.make_async_copy(wide.at[j], sheets.at[s], sems.at[s, 1]),
            )
        )
    copies.append(
        (
            pltpu.make_async_copy(lb_far, lb, sems.at[Z, 0]),
            pltpu.make_async_copy(down_far, down, sems.at[Z, 1]),
        )
    )
    for pair in copies:
        for copy in pair:
            copy.start()
    for s in range(Z):
        for copy in copies[s]:
            copy.wait()
        for half in range(C):
            term = dot(held[s], sheets[s, half], 1, 1)
            total[half] = term if s == 0 else total[half] + term
    for copy in copies[Z]:
        copy.wait()

    mine = core == x_hi
    far[...] = total[1 - core].astype(bf16)
    near[...] = total[jnp.where(mine, 1 - core, core)].astype(bf16)
    for b in range(BLOCKS):
        rows = pl.ds(b * BLOCK, BLOCK)
        term = adapter_scale * dot(lb[rows, RANK:], down[roles[b]], 1, 0)
        part = total[core, rows, :]
        part = jnp.where(mine, part, jnp.zeros_like(part)) + term
        own[rows, :] = jnp.where(live[b] > 0, part, jnp.zeros_like(part))


def arrived_kernel(x, *refs):
    for i in range(refs[-1].shape[0]):
        refs[-1][i] = x[i]


def arrived(x, *blocks):
    return pl.pallas_call(
        arrived_kernel,
        in_specs=[pl.BlockSpec(memory_space=pltpu.SMEM)] + [pl.BlockSpec(memory_space=pl.ANY)] * len(blocks),
        out_specs=pl.BlockSpec(memory_space=pltpu.SMEM),
        out_shape=jax.ShapeDtypeStruct(x.shape, x.dtype),
        cost_estimate=pl.CostEstimate(flops=4 << 30, bytes_accessed=14 << 20, transcendentals=0),
    )(x, *blocks)


def base_parts(place, roles, live, wide, *pieces):
    spec = pltpu.PrefetchScalarGridSpec(
        num_scalar_prefetch=3,
        grid=(1,),
        in_specs=[pl.BlockSpec(memory_space=pl.ANY)] * (1 + len(pieces)),
        out_specs=[pl.BlockSpec((ROWS, COLS), lambda i, p, r, l: (0, 0))] * 3,
        scratch_shapes=[
            pltpu.VMEM((Z, ROWS, COLS), bf16),
            pltpu.VMEM((Z, C, COLS, COLS), bf16),
            pltpu.VMEM((C, ROWS, COLS), f32),
            pltpu.VMEM((ROWS, 2 * RANK), bf16),
            pltpu.VMEM((ROLES, RANK, COLS), bf16),
            pltpu.SemaphoreType.DMA((Z + 1, 2)),
        ],
    )
    return pl.pallas_call(
        base_kernel,
        grid_spec=spec,
        out_shape=[
            jax.ShapeDtypeStruct((ROWS, COLS), bf16),
            jax.ShapeDtypeStruct((ROWS, COLS), bf16),
            jax.ShapeDtypeStruct((ROWS, COLS), f32),
        ],
        compiler_params=pltpu.CompilerParams(vmem_limit_bytes=MOST),
        cost_estimate=pl.CostEstimate(flops=4 * ROWS * COLS * COLS * Z, bytes_accessed=14 << 20, transcendentals=0),
    )(place, roles, live, wide, *pieces)


def shift(x, axis, size, step):
    return lax.ppermute(x, axis, [(i, (i + step) % size) for i in range(size)])


def tie(*values):
    return lax.optimization_barrier(values)


def trade(x, axis, size, bit):
    return lax.ppermute(x, axis, [(i, i ^ bit) for i in range(size)])


def shards(attention_output, grad_out, base_weight, adapter_down, adapter_up, roles, live):
    adapter_down = jnp.transpose(adapter_down, (0, 2, 1))
    tokens = attention_output.shape[0] * Z * XH
    grad_scale = adapter_scale * math.sqrt(ROLES / tokens)
    roles = roles[:, 0]
    place = jnp.stack([lax.axis_index(name) for name in ("z", "xh", "xl", "y", "c")]).astype(jnp.int32)

    wide = lax.all_gather(base_weight, ("z", "c")).reshape(Z, C, COLS, COLS)
    turned = lax.ppermute(grad_out, ("xh", "c"), [(0, 0), (1, 2), (2, 1), (3, 3)])
    ranks = rank_parts(roles, attention_output, grad_out, adapter_down, adapter_up)
    ranks = lax.all_to_all(ranks.reshape(16, ROWS // 16, 2 * RANK), TP, 0, 0)
    ranks, turned = tie(ranks, turned)

    beside = trade(turned, "xl", XL, 1)
    up1, down1 = shift(turned, "y", Y, 1), shift(turned, "y", Y, -1)
    mine = jnp.sum(ranks, axis=0).astype(bf16)
    lb = lax.all_to_all(jnp.broadcast_to(mine[None], (16,) + mine.shape), TP, 0, 0)
    lb, beside, up1, down1 = tie(lb.reshape(ROWS, 2 * RANK), beside, up1, down1)

    up2, beside_down1 = shift(up1, "y", Y, 1), shift(beside, "y", Y, -1)
    outer = outer_parts(roles, live, lb, attention_output, grad_out)
    up2, beside_down1, beside, _ = tie(up2, beside_down1, beside, outer)
    outer = lax.all_to_all(outer, FS, 0, 0)
    beside_up1, beside_down2 = shift(beside, "y", Y, 1), shift(beside_down1, "y", Y, -1)
    pieces = [turned, beside, up1, down1, beside_up1, beside_down1, up2, beside_down2]

    place = arrived(place, up2, beside_up1, beside_down2)
    outer, place = tie(outer, place)
    total = sum_parts(outer, grad_scale)
    other = trade(total, "xh", XH, 1)
    far, near, own = base_parts(place, roles, live, wide, *pieces, lb, adapter_down)
    total, other, far, near, own = tie(total, other, far, near, own)

    far = lax.ppermute(far, ("xh", "c"), [(1, 2), (2, 1)])
    near = lax.ppermute(near, ("xh", "c"), [(0, 1), (1, 3), (2, 0), (3, 2)])
    pair = jnp.where(place[1] == 0, jnp.stack([total, other]), jnp.stack([other, total]))
    s1, t1 = shift(pair, "z", Z, 1), shift(pair, "z", Z, -1)
    s2, t2 = shift(pair, "z", Z, 2), shift(pair, "z", Z, -2)
    s3, t3 = shift(s2, "z", Z, 1), shift(t2, "z", Z, -1)
    s4 = shift(s2, "z", Z, 2)
    token_live = jnp.repeat(live, BLOCK)[:, None] > 0
    input_gradient = jnp.where(token_live, own + far.astype(f32) + near.astype(f32), 0.0).astype(bf16)
    input_gradient, s3, t3, s4 = tie(input_gradient, s3, t3, s4)
    up_gradient, down_gradient = spread(place, [pair, s1, t1, s2, t2, s3, t3, s4])
    return (input_gradient, jnp.transpose(down_gradient, (0, 2, 1)), up_gradient)


def solution(mesh):
    fine = Mesh(mesh.devices.reshape(Z, XH, XL, Y, C), ("z", "xh", "xl", "y", "c"))
    placed = (
        P(FS, TP),
        P(FS, TP),
        P(TP, FS),
        P(None, TP, None),
        P(None, None, TP),
        P(FS, None),
        P(FS),
    )
    return jax.shard_map(
        shards,
        mesh=fine,
        in_specs=placed,
        out_specs=(P(FS, TP), P(None, TP, None), P(None, None, TP)),
        check_vma=False,
    )
```

```python
import functools
import math

import jax
import jax.numpy as jnp
from jax import lax
from jax.experimental import pallas as pl
from jax.experimental.pallas import tpu as pltpu
from jax.sharding import Mesh, PartitionSpec as P

adapter_scale = 2.0
Z, XH, XL, Y, C = 8, 2, 2, 4, 2
FS = ("z", "xh")
TP = ("xl", "y", "c")
ROLES = 8
RANK = 64
BLOCK = 128
BLOCKS = 4
GROUP = RANK // Z
ROWS = 512
COLS = 512
PAD = 128
VMEM = 24 << 20
FULL = 56 << 20
OFFSETS = (0, -1, 1, -2, 2, -3, 3, -4)
MOST = 50 << 20
TILE = 256
f32 = jnp.float32
bf16 = jnp.bfloat16


def dot(a, b, ca, cb):
    return lax.dot_general(a, b, (((ca,), (cb,)), ((), ())), preferred_element_type=f32)


def rank_kernel(roles, att, g, down, up, out):
    for b in range(BLOCKS):
        rows = pl.ds(b * BLOCK, BLOCK)
        out[rows, :RANK] = dot(att[rows, :], down[roles[b]], 1, 1)
        out[rows, RANK:] = dot(g[rows, :], up[roles[b]], 1, 1)


def whole(shape):
    return pl.BlockSpec(shape, lambda i, p: (0,) * len(shape))


def rank_parts(roles, att, g, down, up):
    spec = pltpu.PrefetchScalarGridSpec(
        num_scalar_prefetch=1,
        grid=(1,),
        in_specs=[
            whole((ROWS, COLS)),
            whole((ROWS, COLS)),
            whole((ROLES, RANK, COLS)),
            whole((ROLES, RANK, COLS)),
        ],
        out_specs=whole((ROWS, 2 * RANK)),
    )
    return pl.pallas_call(
        rank_kernel,
        grid_spec=spec,
        out_shape=jax.ShapeDtypeStruct((ROWS, 2 * RANK), f32),
        compiler_params=pltpu.CompilerParams(vmem_limit_bytes=FULL),
        cost_estimate=pl.CostEstimate(flops=2 * 2 * ROWS * COLS * RANK, bytes_accessed=2 << 20, transcendentals=0),
    )(roles, att, g, down, up)


def outer_kernel(roles, live, lb, att_far, g_far, out, att, g, sems):
    copies = []
    for b in range(BLOCKS):
        rows = pl.ds(b * BLOCK, BLOCK)
        pairs = ((g_far.at[rows], g.at[rows]), (att_far.at[rows], att.at[rows]))
        copies.append([pltpu.make_async_copy(x, y, sems.at[b, i]) for i, (x, y) in enumerate(pairs)])
        for copy in copies[b]:
            copy.start()
    for pair in range(BLOCKS // 2):
        ups, downs = [], []
        for b in (2 * pair, 2 * pair + 1):
            rows = pl.ds(b * BLOCK, BLOCK)
            for copy in copies[b]:
                copy.wait()
            ranks = lb[rows, :]
            ranks = jnp.where(live[b] > 0, ranks, jnp.zeros_like(ranks))
            ups.append(dot(ranks[:, :RANK], g[rows, :], 0, 0))
            downs.append(dot(ranks[:, RANK:], att[rows, :], 0, 0))
        at = pl.ds(2 * GROUP * pair, 2 * GROUP)
        first = lax.broadcasted_iota(jnp.int32, (2 * GROUP, PAD), 0) < GROUP
        ids = jnp.where(first, roles[2 * pair], roles[2 * pair + 1])
        ids = ids.astype(f32).astype(bf16)
        for z in range(Z):
            for o, terms in enumerate((ups, downs)):
                part = [t[GROUP * z : GROUP * (z + 1), :] for t in terms]
                out[2 * z + o, at, :COLS] = jnp.concatenate(part, axis=0).astype(bf16)
                out[2 * z + o, at, COLS:] = ids


def outer_parts(roles, live, lb, att, g):
    return pl.pallas_call(
        outer_kernel,
        in_specs=[pl.BlockSpec(memory_space=pltpu.SMEM)] * 2
        + [pl.BlockSpec(memory_space=pltpu.VMEM)]
        + [pl.BlockSpec(memory_space=pl.ANY)] * 2,
        out_specs=pl.BlockSpec(memory_space=pltpu.VMEM),
        scratch_shapes=[
            pltpu.VMEM((ROWS, COLS), bf16),
            pltpu.VMEM((ROWS, COLS), bf16),
            pltpu.SemaphoreType.DMA((BLOCKS, 2)),
        ],
        out_shape=jax.ShapeDtypeStruct((Z * XH, BLOCKS * GROUP, COLS + PAD), bf16),
        compiler_params=pltpu.CompilerParams(vmem_limit_bytes=FULL),
        cost_estimate=pl.CostEstimate(flops=2 * 2 * ROWS * COLS * RANK, bytes_accessed=2 << 20, transcendentals=0),
    )(roles, live, lb, att, g)


def sum_kernel(scale, recv, out):
    got = recv[...]
    shape = (Z * XH * BLOCKS * GROUP, PAD)
    row = lax.broadcasted_iota(jnp.int32, shape, 0)
    lane = lax.broadcasted_iota(jnp.int32, shape, 1)
    role = got[:, COLS:].astype(f32)
    pick = (role == (lane // GROUP).astype(f32)) & (lane % GROUP == row % GROUP)
    total = dot(pick.astype(f32).astype(bf16), got[:, :COLS], 0, 0)
    out[...] = (scale * total[: ROLES * GROUP, :]).astype(bf16)


def sum_parts(recv, scale):
    rows = Z * XH * BLOCKS * GROUP
    return pl.pallas_call(
        functools.partial(sum_kernel, scale),
        out_shape=jax.ShapeDtypeStruct((ROLES * GROUP, COLS), bf16),
        compiler_params=pltpu.CompilerParams(vmem_limit_bytes=16 << 20),
        cost_estimate=pl.CostEstimate(flops=2 * rows * PAD * COLS, bytes_accessed=2 << 20, transcendentals=0),
    )(recv.reshape(rows, COLS + PAD))


def spread_kernel(place, *refs):
    pieces, up, down = refs[:Z], refs[Z], refs[Z + 1]
    for off, piece in zip(OFFSETS, pieces):
        z = lax.rem(place[0] + (off + Z), Z)
        at = pl.ds(pl.multiple_of(GROUP * z, GROUP), GROUP)
        for o, out in enumerate((up, down)):
            rows = piece[o].astype(f32)
            for k in range(ROLES):
                out[k, at, :] = rows[GROUP * k : GROUP * (k + 1), :]


def spread(place, pieces):
    spec = pltpu.PrefetchScalarGridSpec(
        num_scalar_prefetch=1,
        grid=(1,),
        in_specs=[whole((2, ROLES * GROUP, COLS))] * Z,
        out_specs=[whole((ROLES, RANK, COLS))] * 2,
    )
    return pl.pallas_call(
        spread_kernel,
        grid_spec=spec,
        out_shape=[jax.ShapeDtypeStruct((ROLES, RANK, COLS), f32)] * 2,
        compiler_params=pltpu.CompilerParams(vmem_limit_bytes=VMEM),
        cost_estimate=pl.CostEstimate(flops=0, bytes_accessed=4 << 20, transcendentals=0),
    )(place, *pieces)


def base_kernel(place, roles, live, wide, *refs):
    pieces, (lb_far, down_far), (far, near, own) = refs[:Z], refs[Z : Z + 2], refs[Z + 2 : Z + 5]
    held, sheets, total, lb, down, sems = refs[Z + 5 :]
    x_hi, x_lo, y, core = place[1], place[2], place[3], place[4]
    columns = (x_lo, 1 - x_lo, x_lo, x_lo, 1 - x_lo, 1 - x_lo, x_lo, 1 - x_lo)
    steps = (0, 0, -1, 1, -1, 1, 2, 2)
    copies = []
    for s, (piece, column, step) in enumerate(zip(pieces, columns, steps)):
        j = column * Y + lax.rem(y + Y + step, Y)
        copies.append(
            (
                pltpu.make_async_copy(piece, held.at[s], sems.at[s, 0]),
                pltpu.make_async_copy(wide.at[j], sheets.at[s], sems.at[s, 1]),
            )
        )
    copies.append(
        (
            pltpu.make_async_copy(lb_far, lb, sems.at[Z, 0]),
            pltpu.make_async_copy(down_far, down, sems.at[Z, 1]),
        )
    )
    for pair in copies:
        for copy in pair:
            copy.start()
    for s in range(Z):
        for copy in copies[s]:
            copy.wait()
        for half in range(C):
            term = dot(held[s], sheets[s, half], 1, 1)
            total[half] = term if s == 0 else total[half] + term
    for copy in copies[Z]:
        copy.wait()

    mine = core == x_hi
    far[...] = total[1 - core].astype(bf16)
    near[...] = total[jnp.where(mine, 1 - core, core)].astype(bf16)
    for b in range(BLOCKS):
        rows = pl.ds(b * BLOCK, BLOCK)
        term = adapter_scale * dot(lb[rows, RANK:], down[roles[b]], 1, 0)
        part = total[core, rows, :]
        part = jnp.where(mine, part, jnp.zeros_like(part)) + term
        own[rows, :] = jnp.where(live[b] > 0, part, jnp.zeros_like(part))


def arrived_kernel(x, *refs):
    for i in range(refs[-1].shape[0]):
        refs[-1][i] = x[i]


def arrived(x, *blocks):
    return pl.pallas_call(
        arrived_kernel,
        in_specs=[pl.BlockSpec(memory_space=pltpu.SMEM)] + [pl.BlockSpec(memory_space=pl.ANY)] * len(blocks),
        out_specs=pl.BlockSpec(memory_space=pltpu.SMEM),
        out_shape=jax.ShapeDtypeStruct(x.shape, x.dtype),
        cost_estimate=pl.CostEstimate(flops=4 << 30, bytes_accessed=14 << 20, transcendentals=0),
    )(x, *blocks)


def base_parts(place, roles, live, wide, *pieces):
    spec = pltpu.PrefetchScalarGridSpec(
        num_scalar_prefetch=3,
        grid=(1,),
        in_specs=[pl.BlockSpec(memory_space=pl.ANY)] * (1 + len(pieces)),
        out_specs=[pl.BlockSpec((ROWS, COLS), lambda i, p, r, l: (0, 0))] * 3,
        scratch_shapes=[
            pltpu.VMEM((Z, ROWS, COLS), bf16),
            pltpu.VMEM((Z, C, COLS, COLS), bf16),
            pltpu.VMEM((C, ROWS, COLS), f32),
            pltpu.VMEM((ROWS, 2 * RANK), bf16),
            pltpu.VMEM((ROLES, RANK, COLS), bf16),
            pltpu.SemaphoreType.DMA((Z + 1, 2)),
        ],
    )
    return pl.pallas_call(
        base_kernel,
        grid_spec=spec,
        out_shape=[
            jax.ShapeDtypeStruct((ROWS, COLS), bf16),
            jax.ShapeDtypeStruct((ROWS, COLS), bf16),
            jax.ShapeDtypeStruct((ROWS, COLS), f32),
        ],
        compiler_params=pltpu.CompilerParams(vmem_limit_bytes=MOST),
        cost_estimate=pl.CostEstimate(flops=4 * ROWS * COLS * COLS * Z, bytes_accessed=14 << 20, transcendentals=0),
    )(place, roles, live, wide, *pieces)


def shift(x, axis, size, step):
    return lax.ppermute(x, axis, [(i, (i + step) % size) for i in range(size)])


def tie(*values):
    return lax.optimization_barrier(values)


def trade(x, axis, size, bit):
    return lax.ppermute(x, axis, [(i, i ^ bit) for i in range(size)])


def shards(attention_output, grad_out, base_weight, adapter_down, adapter_up, roles, live):
    adapter_down = jnp.transpose(adapter_down, (0, 2, 1))
    tokens = attention_output.shape[0] * Z * XH
    grad_scale = adapter_scale * math.sqrt(ROLES / tokens)
    roles = roles[:, 0]
    place = jnp.stack([lax.axis_index(name) for name in ("z", "xh", "xl", "y", "c")]).astype(jnp.int32)

    wide = lax.all_gather(base_weight, ("z", "c")).reshape(Z, C, COLS, COLS)
    turned = lax.ppermute(grad_out, ("xh", "c"), [(0, 0), (1, 2), (2, 1), (3, 3)])
    ranks = rank_parts(roles, attention_output, grad_out, adapter_down, adapter_up)
    ranks = lax.all_to_all(ranks.reshape(16, ROWS // 16, 2 * RANK), TP, 0, 0)
    ranks, turned = tie(ranks, turned)

    beside = trade(turned, "xl", XL, 1)
    up1, down1 = shift(turned, "y", Y, 1), shift(turned, "y", Y, -1)
    mine = jnp.sum(ranks, axis=0).astype(bf16)
    lb = lax.all_to_all(jnp.broadcast_to(mine[None], (16,) + mine.shape), TP, 0, 0)
    lb, beside, up1, down1 = tie(lb.reshape(ROWS, 2 * RANK), beside, up1, down1)

    up2, beside_down1 = shift(up1, "y", Y, 1), shift(beside, "y", Y, -1)
    outer = outer_parts(roles, live, lb, attention_output, grad_out)
    up2, beside_down1, beside, _ = tie(up2, beside_down1, beside, outer)
    outer = lax.all_to_all(outer, FS, 0, 0)
    beside_up1, beside_down2 = shift(beside, "y", Y, 1), shift(beside_down1, "y", Y, -1)

    beside_up1, beside_down2 = tie(beside_up1, beside_down2)
    mark = arrived(place, beside_down2)
    outer, mark = tie(outer, mark)
    total = sum_parts(outer, grad_scale)
    other = trade(total, "xh", XH, 1)
    pieces = [turned, beside, up1, down1, beside_up1, beside_down1, up2, beside_down2]
    far, near, own = base_parts(place, roles, live, wide, *pieces, lb, adapter_down)
    total, other, far, near, own = tie(total, other, far, near, own)

    far = lax.ppermute(far, ("xh", "c"), [(1, 2), (2, 1)])
    near = lax.ppermute(near, ("xh", "c"), [(0, 1), (1, 3), (2, 0), (3, 2)])
    pair = jnp.where(place[1] == 0, jnp.stack([total, other]), jnp.stack([other, total]))
    s1, t1 = shift(pair, "z", Z, 1), shift(pair, "z", Z, -1)
    s2, t2 = shift(pair, "z", Z, 2), shift(pair, "z", Z, -2)
    s3, t3 = shift(s2, "z", Z, 1), shift(t2, "z", Z, -1)
    s4 = shift(s2, "z", Z, 2)
    token_live = jnp.repeat(live, BLOCK)[:, None] > 0
    input_gradient = jnp.where(token_live, own + far.astype(f32) + near.astype(f32), 0.0).astype(bf16)
    input_gradient, s3, t3, s4 = tie(input_gradient, s3, t3, s4)
    up_gradient, down_gradient = spread(mark, [pair, s1, t1, s2, t2, s3, t3, s4])
    return (input_gradient, jnp.transpose(down_gradient, (0, 2, 1)), up_gradient)


def solution(mesh):
    fine = Mesh(mesh.devices.reshape(Z, XH, XL, Y, C), ("z", "xh", "xl", "y", "c"))
    placed = (
        P(FS, TP),
        P(FS, TP),
        P(TP, FS),
        P(None, TP, None),
        P(None, None, TP),
        P(FS, None),
        P(FS),
    )
    return jax.shard_map(
        shards,
        mesh=fine,
        in_specs=placed,
        out_specs=(P(FS, TP), P(None, TP, None), P(None, None, TP)),
        check_vma=False,
    )
```

```python
import functools
import math

import jax
import jax.numpy as jnp
from jax import lax
from jax.experimental import pallas as pl
from jax.experimental.pallas import tpu as pltpu
from jax.sharding import Mesh, PartitionSpec as P

adapter_scale = 2.0
Z, XH, XL, Y, C = 8, 2, 2, 4, 2
FS = ("z", "xh")
TP = ("xl", "y", "c")
ROLES = 8
RANK = 64
BLOCK = 128
BLOCKS = 4
GROUP = RANK // Z
ROWS = 512
COLS = 512
LANES = 128
IDS = 8
VMEM = 24 << 20
FULL = 56 << 20
OFFSETS = (0, -1, 1, -2, 2, -3, 3, -4)
MOST = 50 << 20
TILE = 256
f32 = jnp.float32
bf16 = jnp.bfloat16


def dot(a, b, ca, cb):
    return lax.dot_general(a, b, (((ca,), (cb,)), ((), ())), preferred_element_type=f32)


def rank_kernel(roles, att, g, down, up, out):
    for b in range(BLOCKS):
        rows = pl.ds(b * BLOCK, BLOCK)
        out[rows, :RANK] = dot(att[rows, :], down[roles[b]], 1, 1)
        out[rows, RANK:] = dot(g[rows, :], up[roles[b]], 1, 1)


def whole(shape):
    return pl.BlockSpec(shape, lambda i, p: (0,) * len(shape))


def rank_parts(roles, att, g, down, up):
    spec = pltpu.PrefetchScalarGridSpec(
        num_scalar_prefetch=1,
        grid=(1,),
        in_specs=[
            whole((ROWS, COLS)),
            whole((ROWS, COLS)),
            whole((ROLES, RANK, COLS)),
            whole((ROLES, RANK, COLS)),
        ],
        out_specs=whole((ROWS, 2 * RANK)),
    )
    return pl.pallas_call(
        rank_kernel,
        grid_spec=spec,
        out_shape=jax.ShapeDtypeStruct((ROWS, 2 * RANK), f32),
        compiler_params=pltpu.CompilerParams(vmem_limit_bytes=FULL),
        cost_estimate=pl.CostEstimate(flops=2 * 2 * ROWS * COLS * RANK, bytes_accessed=2 << 20, transcendentals=0),
    )(roles, att, g, down, up)


def outer_kernel(live, lb, att_far, g_far, out, att, g, sems):
    copies = []
    for b in range(BLOCKS):
        rows = pl.ds(b * BLOCK, BLOCK)
        pairs = ((g_far.at[rows], g.at[rows]), (att_far.at[rows], att.at[rows]))
        copies.append([pltpu.make_async_copy(x, y, sems.at[b, i]) for i, (x, y) in enumerate(pairs)])
        for copy in copies[b]:
            copy.start()
    for pair in range(BLOCKS // 2):
        ups, downs = [], []
        for b in (2 * pair, 2 * pair + 1):
            rows = pl.ds(b * BLOCK, BLOCK)
            for copy in copies[b]:
                copy.wait()
            ranks = lb[rows, :]
            ranks = jnp.where(live[b] > 0, ranks, jnp.zeros_like(ranks))
            ups.append(dot(ranks[:, :RANK], g[rows, :], 0, 0))
            downs.append(dot(ranks[:, RANK:], att[rows, :], 0, 0))
        at = pl.ds(2 * GROUP * pair, 2 * GROUP)
        for z in range(Z):
            for o, terms in enumerate((ups, downs)):
                part = [t[GROUP * z : GROUP * (z + 1), :] for t in terms]
                out[2 * z + o, at, :] = jnp.concatenate(part, axis=0).astype(bf16)


def outer_parts(live, lb, att, g):
    return pl.pallas_call(
        outer_kernel,
        in_specs=[pl.BlockSpec(memory_space=pltpu.SMEM), pl.BlockSpec(memory_space=pltpu.VMEM)]
        + [pl.BlockSpec(memory_space=pl.ANY)] * 2,
        out_specs=pl.BlockSpec(memory_space=pltpu.VMEM),
        scratch_shapes=[
            pltpu.VMEM((ROWS, COLS), bf16),
            pltpu.VMEM((ROWS, COLS), bf16),
            pltpu.SemaphoreType.DMA((BLOCKS, 2)),
        ],
        out_shape=jax.ShapeDtypeStruct((Z * XH, BLOCKS * GROUP, COLS), bf16),
        compiler_params=pltpu.CompilerParams(vmem_limit_bytes=FULL),
        cost_estimate=pl.CostEstimate(flops=2 * 2 * ROWS * COLS * RANK, bytes_accessed=2 << 20, transcendentals=0),
    )(live, lb, att, g)


def sum_kernel(scale, place, got, ids, out):
    lane = lax.broadcasted_iota(jnp.int32, (GROUP, LANES), 1)
    row = lax.broadcasted_iota(jnp.int32, (GROUP, LANES), 0)
    rank = lane % GROUP == row
    wanted = (lane // GROUP).astype(f32)
    pick = []
    for z in range(Z):
        for h in range(XH):
            theirs = ids[(place[0] ^ z) * XH + (place[1] ^ h)]
            for b in range(BLOCKS):
                at = IDS // BLOCKS * b
                role = jnp.broadcast_to(theirs[at : at + 1, :], (GROUP, LANES))
                pick.append(jnp.where(rank & (role == wanted), 1.0, 0.0))
    pick = jnp.concatenate(pick, axis=0).astype(bf16)
    total = dot(pick, got[...], 0, 0)
    out[...] = (scale * total[: ROLES * GROUP, :]).astype(bf16)


def sum_parts(place, recv, ids, scale):
    rows = Z * XH * BLOCKS * GROUP
    here = pl.BlockSpec(memory_space=pltpu.VMEM)
    return pl.pallas_call(
        functools.partial(sum_kernel, scale),
        in_specs=[pl.BlockSpec(memory_space=pltpu.SMEM)] + [here] * 2,
        out_specs=here,
        out_shape=jax.ShapeDtypeStruct((ROLES * GROUP, COLS), bf16),
        compiler_params=pltpu.CompilerParams(vmem_limit_bytes=16 << 20),
        cost_estimate=pl.CostEstimate(flops=2 * rows * LANES * COLS, bytes_accessed=2 << 20, transcendentals=0),
    )(place, recv.reshape(rows, COLS), ids)


def spread_kernel(place, *refs):
    pieces, up, down = refs[:Z], refs[Z], refs[Z + 1]
    for off, piece in zip(OFFSETS, pieces):
        z = lax.rem(place[0] + (off + Z), Z)
        at = pl.ds(pl.multiple_of(GROUP * z, GROUP), GROUP)
        for o, out in enumerate((up, down)):
            rows = piece[o].astype(f32)
            for k in range(ROLES):
                out[k, at, :] = rows[GROUP * k : GROUP * (k + 1), :]


def spread(place, pieces):
    spec = pltpu.PrefetchScalarGridSpec(
        num_scalar_prefetch=1,
        grid=(1,),
        in_specs=[whole((2, ROLES * GROUP, COLS))] * Z,
        out_specs=[whole((ROLES, RANK, COLS))] * 2,
    )
    return pl.pallas_call(
        spread_kernel,
        grid_spec=spec,
        out_shape=[jax.ShapeDtypeStruct((ROLES, RANK, COLS), f32)] * 2,
        compiler_params=pltpu.CompilerParams(vmem_limit_bytes=VMEM),
        cost_estimate=pl.CostEstimate(flops=0, bytes_accessed=4 << 20, transcendentals=0),
    )(place, *pieces)


def base_kernel(place, roles, live, wide, *refs):
    pieces, (lb_far, down_far), (far, near, own) = refs[:Z], refs[Z : Z + 2], refs[Z + 2 : Z + 5]
    held, sheets, total, lb, down, sems = refs[Z + 5 :]
    x_hi, x_lo, y, core = place[1], place[2], place[3], place[4]
    columns = (x_lo, 1 - x_lo, x_lo, x_lo, 1 - x_lo, 1 - x_lo, x_lo, 1 - x_lo)
    steps = (0, 0, -1, 1, -1, 1, 2, 2)
    copies = []
    for s, (piece, column, step) in enumerate(zip(pieces, columns, steps)):
        j = column * Y + lax.rem(y + Y + step, Y)
        copies.append(
            (
                pltpu.make_async_copy(piece, held.at[s], sems.at[s, 0]),
                pltpu.make_async_copy(wide.at[j], sheets.at[s], sems.at[s, 1]),
            )
        )
    copies.append(
        (
            pltpu.make_async_copy(lb_far, lb, sems.at[Z, 0]),
            pltpu.make_async_copy(down_far, down, sems.at[Z, 1]),
        )
    )
    for pair in copies:
        for copy in pair:
            copy.start()
    for s in range(Z):
        for copy in copies[s]:
            copy.wait()
        for half in range(C):
            term = dot(held[s], sheets[s, half], 1, 1)
            total[half] = term if s == 0 else total[half] + term
    for copy in copies[Z]:
        copy.wait()

    mine = core == x_hi
    far[...] = total[1 - core].astype(bf16)
    near[...] = total[jnp.where(mine, 1 - core, core)].astype(bf16)
    for b in range(BLOCKS):
        rows = pl.ds(b * BLOCK, BLOCK)
        term = adapter_scale * dot(lb[rows, RANK:], down[roles[b]], 1, 0)
        part = total[core, rows, :]
        part = jnp.where(mine, part, jnp.zeros_like(part)) + term
        own[rows, :] = jnp.where(live[b] > 0, part, jnp.zeros_like(part))


def arrived_kernel(x, *refs):
    for i in range(refs[-1].shape[0]):
        refs[-1][i] = x[i]


def arrived(x, *blocks):
    return pl.pallas_call(
        arrived_kernel,
        in_specs=[pl.BlockSpec(memory_space=pltpu.SMEM)] + [pl.BlockSpec(memory_space=pl.ANY)] * len(blocks),
        out_specs=pl.BlockSpec(memory_space=pltpu.SMEM),
        out_shape=jax.ShapeDtypeStruct(x.shape, x.dtype),
        cost_estimate=pl.CostEstimate(flops=4 << 30, bytes_accessed=14 << 20, transcendentals=0),
    )(x, *blocks)


def base_parts(place, roles, live, wide, *pieces):
    spec = pltpu.PrefetchScalarGridSpec(
        num_scalar_prefetch=3,
        grid=(1,),
        in_specs=[pl.BlockSpec(memory_space=pl.ANY)] * (1 + len(pieces)),
        out_specs=[pl.BlockSpec((ROWS, COLS), lambda i, p, r, l: (0, 0))] * 3,
        scratch_shapes=[
            pltpu.VMEM((Z, ROWS, COLS), bf16),
            pltpu.VMEM((Z, C, COLS, COLS), bf16),
            pltpu.VMEM((C, ROWS, COLS), f32),
            pltpu.VMEM((ROWS, 2 * RANK), bf16),
            pltpu.VMEM((ROLES, RANK, COLS), bf16),
            pltpu.SemaphoreType.DMA((Z + 1, 2)),
        ],
    )
    return pl.pallas_call(
        base_kernel,
        grid_spec=spec,
        out_shape=[
            jax.ShapeDtypeStruct((ROWS, COLS), bf16),
            jax.ShapeDtypeStruct((ROWS, COLS), bf16),
            jax.ShapeDtypeStruct((ROWS, COLS), f32),
        ],
        compiler_params=pltpu.CompilerParams(vmem_limit_bytes=MOST),
        cost_estimate=pl.CostEstimate(flops=4 * ROWS * COLS * COLS * Z, bytes_accessed=14 << 20, transcendentals=0),
    )(place, roles, live, wide, *pieces)


def shift(x, axis, size, step):
    return lax.ppermute(x, axis, [(i, (i + step) % size) for i in range(size)])


def tie(*values):
    return lax.optimization_barrier(values)


def trade(x, axis, size, bit):
    return lax.ppermute(x, axis, [(i, i ^ bit) for i in range(size)])


def shards(attention_output, grad_out, base_weight, adapter_down, adapter_up, roles, live):
    adapter_down = jnp.transpose(adapter_down, (0, 2, 1))
    tokens = attention_output.shape[0] * Z * XH
    grad_scale = adapter_scale * math.sqrt(ROLES / tokens)
    roles = roles[:, 0]
    place = jnp.stack([lax.axis_index(name) for name in ("z", "xh", "xl", "y", "c")]).astype(jnp.int32)

    wide = lax.all_gather(base_weight, ("z", "c")).reshape(Z, C, COLS, COLS)
    turned = lax.ppermute(grad_out, ("xh", "c"), [(0, 0), (1, 2), (2, 1), (3, 3)])
    ranks = rank_parts(roles, attention_output, grad_out, adapter_down, adapter_up)
    ranks = lax.all_to_all(ranks.reshape(16, ROWS // 16, 2 * RANK), TP, 0, 0)
    ids = jnp.broadcast_to(jnp.repeat(roles, IDS // BLOCKS)[:, None], (IDS, LANES)).astype(f32)
    other = trade(ids, "xh", XH, 1)
    ranks, turned, other = tie(ranks, turned, other)
    ids = jnp.stack([ids, other])
    ids = jnp.concatenate([ids] + [trade(ids, "z", Z, bits) for bits in (1, 2, 3)])

    beside = trade(turned, "xl", XL, 1)
    up1, down1 = shift(turned, "y", Y, 1), shift(turned, "y", Y, -1)
    mine = jnp.sum(ranks, axis=0).astype(bf16)
    lb = lax.all_to_all(jnp.broadcast_to(mine[None], (16,) + mine.shape), TP, 0, 0)
    lb, beside, up1, down1, ids = tie(lb.reshape(ROWS, 2 * RANK), beside, up1, down1, ids)
    ids = jnp.concatenate([ids, trade(ids, "z", Z, 4)])

    up2, beside_down1 = shift(up1, "y", Y, 1), shift(beside, "y", Y, -1)
    outer = outer_parts(live, lb, attention_output, grad_out)
    up2, beside_down1, beside, ids, _ = tie(up2, beside_down1, beside, ids, outer)
    outer = lax.all_to_all(outer, FS, 0, 0)
    beside_up1, beside_down2 = shift(beside, "y", Y, 1), shift(beside_down1, "y", Y, -1)

    beside_up1, beside_down2 = tie(beside_up1, beside_down2)
    mark = arrived(place, beside_down2)
    outer, mark, ids = tie(outer, mark, ids)
    total = sum_parts(place, outer, ids, grad_scale)
    other = trade(total, "xh", XH, 1)
    pieces = [turned, beside, up1, down1, beside_up1, beside_down1, up2, beside_down2]
    far, near, own = base_parts(place, roles, live, wide, *pieces, lb, adapter_down)
    total, other, far, near, own = tie(total, other, far, near, own)

    far = lax.ppermute(far, ("xh", "c"), [(1, 2), (2, 1)])
    near = lax.ppermute(near, ("xh", "c"), [(0, 1), (1, 3), (2, 0), (3, 2)])
    pair = jnp.where(place[1] == 0, jnp.stack([total, other]), jnp.stack([other, total]))
    s1, t1 = shift(pair, "z", Z, 1), shift(pair, "z", Z, -1)
    s2, t2 = shift(pair, "z", Z, 2), shift(pair, "z", Z, -2)
    s3, t3 = shift(s2, "z", Z, 1), shift(t2, "z", Z, -1)
    s4 = shift(s2, "z", Z, 2)
    token_live = jnp.repeat(live, BLOCK)[:, None] > 0
    input_gradient = jnp.where(token_live, own + far.astype(f32) + near.astype(f32), 0.0).astype(bf16)
    input_gradient, s3, t3, s4 = tie(input_gradient, s3, t3, s4)
    up_gradient, down_gradient = spread(mark, [pair, s1, t1, s2, t2, s3, t3, s4])
    return (input_gradient, jnp.transpose(down_gradient, (0, 2, 1)), up_gradient)


def solution(mesh):
    fine = Mesh(mesh.devices.reshape(Z, XH, XL, Y, C), ("z", "xh", "xl", "y", "c"))
    placed = (
        P(FS, TP),
        P(FS, TP),
        P(TP, FS),
        P(None, TP, None),
        P(None, None, TP),
        P(FS, None),
        P(FS),
    )
    return jax.shard_map(
        shards,
        mesh=fine,
        in_specs=placed,
        out_specs=(P(FS, TP), P(None, TP, None), P(None, None, TP)),
        check_vma=False,
    )
```
